512 devices in a mesh: dp: 8 (over y, core), expert: 32 (over z, x_hi), tensor: 2 (over x_lo).
Axes of the slice: x: 4 (x_hi: 2, x_lo: 2; x = x_hi * 2 + x_lo), y: 4, z: 16, core: 2. Of those that a mesh axis runs over, the one named last changes fastest.
Arguments:
- states: bfloat16 [8192, 4096], P(('dp', 'expert'), 'tensor'), parts along dimension 0, may hold values from -512 to 512
- norm_gain: float32 [4096], P('tensor'), may hold values from 0.1 to 1.9
- expert_ids: int32 [8192, 8], P(('dp', 'expert')), parts along dimension 0, may hold values from 0 to 127, as said below
- route_gates: float32 [8192, 8], P(('dp', 'expert')), parts along dimension 0, may hold values from 0.1 to 1
- w_gate: bfloat16 [32, 4096, 384], P('expert', 'tensor'), may hold values from -0.09375 to 0.09375
- w_up: bfloat16 [32, 4096, 384], P('expert', 'tensor'), may hold values from -0.09375 to 0.09375
- w_down: bfloat16 [32, 384, 4096], P('expert', None, 'tensor'), may hold values from -0.15625 to 0.15625
Outputs:
- mixture: bfloat16 [8192, 4096], P(('dp', 'expert'), 'tensor'), parts along dimension 0
The draws below stay inside these ranges and needn't reach their ends.
There are 8 independent parts, one for each index of `dp`. The reference program is written for one: setup_inputs(seed, part) draws one part's arguments, and reference() takes and returns one part's arrays. A program takes and returns all parts, laid end to end along the dimension named above; an argument that names none is the same for every part. Nothing has to cross between parts.
Inputs may be any that keep to these rules, and one draw needn't show every extreme that they name: `expert_ids`: each row names 8 different experts. Among the 32 rows of one index of expert (aligned blocks), each expert below 8 is named by at most 16 rows, and in every draw some expert below 8 is named by exactly 16 rows in every block.
All inputs are finite; a program needn't handle non-finite values.
Results may differ from the reference program's by a relative error of at most 0.014.
Values may be sent and summed in bfloat16 or wider, within the bound.
No kernel may reach another device: no remote copies, remote signals or barrier semaphores. Data moves between devices by JAX's collectives and lax.ppermute only.
A program may use at most 64 MiB of HBM per device.

```python
import math
import jax
import jax.numpy as jnp
from jax import lax

D = 4096
EXPERTS = 128
TOPK = 8
GROUP = 4
FW_DEV = 384
TOK_DEV = 32
FW = 1536
EF = 8
SLICES = 32
CAP = 16
TOKENS = 1024
N_EXPERT = 32


def draw_states(key, part):
    key = jax.random.fold_in(key, 5)
    subkeys = jax.random.split(key, 3)
    base_draw = jax.random.truncated_normal(subkeys[0], -4.0, 4.0, (TOKENS, D), jnp.float32)
    row_scale = jnp.exp(jax.random.uniform(subkeys[1], (TOKENS, 1), jnp.float32, 0.0, math.log(10.0)))
    col_scale = jnp.exp(jnp.arange(D, dtype=jnp.float32)[None, :] * (math.log(10.0) / D))
    col_scale = col_scale * jnp.exp(jax.random.uniform(subkeys[2], (1, D), jnp.float32, 0.0, math.log(2.0)))
    return jnp.clip(base_draw * row_scale * col_scale, -512.0, 512.0).astype(jnp.bfloat16)


def draw_expert_ids(key, part):
    key = jax.random.fold_in(key, 11)
    subkeys = jax.random.split(key, 4)
    blocks = TOKENS // TOK_DEV
    full_one = jax.random.randint(subkeys[0], (), 0, EF)
    counts = jax.random.randint(subkeys[1], (blocks, EF), CAP // 2, CAP + 1)
    counts = jnp.where(jnp.arange(EF)[None, :] == full_one, CAP, counts)
    noise_bits = jax.random.randint(subkeys[2], (blocks, EF, TOK_DEV), 0, 1 << 20)
    scores = noise_bits * TOK_DEV + jnp.arange(TOK_DEV, dtype=jnp.int32)[None, None, :]
    row_ranks = jnp.argsort(jnp.argsort(scores, axis=2), axis=2)
    member = row_ranks < counts[:, :, None]
    member = member.transpose(0, 2, 1).reshape(TOKENS, EF)
    others = jax.random.randint(subkeys[3], (TOKENS, EXPERTS - EF), 0, 1 << 20) * EXPERTS
    others = others + jnp.arange(EXPERTS - EF, dtype=jnp.int32)[None, :]
    flight_ids = jnp.arange(EF, dtype=jnp.int32)[None, :]
    inside = jnp.where(member, (1 << 29) + flight_ids, -1 - flight_ids)
    scored = jnp.concatenate([inside, others], axis=1)
    return lax.top_k(scored, TOPK)[1].astype(jnp.int32)


def levels(stream_key, extent, cuts, low, largest):
    gain, own = 1.0, jax.random.fold_in(stream_key, 6)
    for dim, blocks in cuts:
        steps = jnp.exp(jax.random.uniform(jax.random.fold_in(own, dim), (blocks,), jnp.float32, low / len(cuts), largest / len(cuts)))
        gain = gain * jnp.repeat(steps, extent[dim] // blocks).reshape([-1 if axis == dim else 1 for axis in range(len(extent))])
    return gain


def noise(rng, extent, spread, most, pieces=(), kind=jnp.bfloat16):
    level = levels(rng, extent, pieces, -0.22, 0.18) if pieces else 1.0
    array = jax.random.normal(rng, extent, jnp.float32) * spread * level
    return jnp.minimum(jnp.maximum(array, -most), most).astype(kind)


def setup_inputs(seed: int = 0, part: int = 0) -> dict:
    splits = jax.random.split(jax.random.key(seed), 8)
    part_splits = jax.random.split(jax.random.fold_in(splits[7], part), 8)
    return {
        "states": draw_states(jax.random.fold_in(jax.random.fold_in(splits[7], part), 71), part),
        "norm_gain": jnp.clip(1.0 + 0.18 * jax.random.normal(splits[1], (D,), jnp.float32), 0.1, 1.9),
        "expert_ids": draw_expert_ids(jax.random.fold_in(jax.random.fold_in(splits[7], part), 71), part),
        "route_gates": jnp.clip(0.1 + 0.9 * jax.random.uniform(part_splits[3], (TOKENS, TOPK), jnp.float32) ** levels(part_splits[3], (TOKENS, TOPK), ((0, 32),), -0.2, 0.2), 0.1, 1.0),
        "w_gate": noise(splits[4], (SLICES, D, FW_DEV), D ** -0.5, 0.09375, ((0, 32), (1, 2))),
        "w_up": noise(splits[5], (SLICES, D, FW_DEV), D ** -0.5, 0.09375, ((0, 32), (1, 2))),
        "w_down": noise(splits[6], (SLICES, FW_DEV, D), FW ** -0.5, 0.15625, ((0, 32), (2, 2))),
    }


EPSILON = 1e-06

def reference(states, norm_gain, expert_ids, route_gates, w_gate, w_up, w_down):
    values = states.astype(jnp.float32)
    mean_sq = lax.optimization_barrier(jnp.mean(values * values, axis=1))
    normed = (values * lax.rsqrt(mean_sq + EPSILON)[:, None] * norm_gain[None, :]).astype(jnp.bfloat16)
    gate_full = w_gate.reshape(EF, GROUP, D, FW_DEV).transpose(0, 2, 1, 3).reshape(EF, D, FW)
    up_full = w_up.reshape(EF, GROUP, D, FW_DEV).transpose(0, 2, 1, 3).reshape(EF, D, FW)
    down_full = w_down.reshape(EF, FW, D)
    row_limit = CAP * N_EXPERT
    accumulated = jnp.zeros((TOKENS, D), jnp.float32)
    for expert in range(EF):
        matches = expert_ids == expert
        member = jnp.any(matches, axis=1)
        weight = lax.optimization_barrier(jnp.sum(jnp.where(matches, route_gates, 0.0), axis=1))
        chosen = jnp.nonzero(member, size=row_limit, fill_value=0)[0].astype(jnp.int32)
        is_live = jnp.arange(row_limit) < jnp.sum(member.astype(jnp.int32))
        selected = normed[chosen]
        gate_val = jnp.dot(selected, gate_full[expert], preferred_element_type=jnp.float32)
        up_val = jnp.dot(selected, up_full[expert], preferred_element_type=jnp.float32)
        hidden = (jax.nn.silu(gate_val) * up_val).astype(jnp.bfloat16)
        output = jnp.dot(hidden, down_full[expert], preferred_element_type=jnp.float32).astype(jnp.bfloat16)
        scaled = jnp.where(is_live, weight[chosen], 0.0)[:, None] * output.astype(jnp.float32)
        accumulated = accumulated.at[chosen].add(scaled)
    return accumulated.astype(jnp.bfloat16)
```

```python
import jax
import jax.numpy as jnp
from jax import lax
from jax.sharding import Mesh, PartitionSpec as P

D = 4096
GROUP = 4
EPSILON = 1e-06
SWAP = [(0, 1), (1, 0)]


def shards(states, norm_gain, expert_ids, route_gates, w_gate, w_up, w_down):
    tokens, width = states.shape
    units = w_gate.shape[2]
    depth = lax.axis_size("z")
    replicas = lax.axis_size("y") * lax.axis_size("core")
    experts = depth * lax.axis_size("xh") // GROUP
    spread = depth // experts
    capacity = tokens // 2
    rows = depth * capacity

    replica = lax.axis_index("y") * lax.axis_size("core") + lax.axis_index("core")
    share, down_share = width // replicas, units // replicas
    mine = jnp.concatenate(
        [
            lax.dynamic_slice_in_dim(w_gate[0], replica * share, share, 0),
            lax.dynamic_slice_in_dim(w_up[0], replica * share, share, 0),
        ],
        axis=1,
    )
    mine_down = lax.dynamic_slice_in_dim(w_down[0], replica * down_share, down_share, 0)
    other = lax.ppermute(mine, "xh", SWAP)
    other_down = lax.ppermute(mine_down, "xh", SWAP)
    w_in_other = lax.all_gather(other, ("y", "core"), axis=0, tiled=True)
    w_down_other = lax.all_gather(other_down, ("y", "core"), axis=0, tiled=True)

    flight_ids = jnp.arange(experts, dtype=jnp.int32)
    matches = expert_ids[:, :, None] == flight_ids[None, None, :]
    member = jnp.any(matches, axis=1)
    weight = jnp.sum(jnp.where(matches, route_gates[:, :, None], 0.0), axis=1)
    before = jnp.tril(jnp.ones((tokens, tokens), jnp.float32), -1)
    position = jnp.dot(before, member.astype(jnp.float32)).astype(jnp.int32)
    slots = jnp.where(member, position, capacity)
    slots = jnp.repeat(slots, spread, axis=1)
    slot_ids = jnp.arange(capacity, dtype=jnp.int32)
    placed = slots.T[:, None, :] == slot_ids[None, :, None]
    placed = placed.reshape(rows, tokens)
    packed = jnp.dot(
        placed.astype(jnp.bfloat16), states, preferred_element_type=jnp.float32
    ).astype(jnp.bfloat16)
    arrived = lax.all_to_all(
        packed.reshape(depth, capacity, width), "z", split_axis=0, concat_axis=0, tiled=True
    ).reshape(rows, width)

    values = arrived.astype(jnp.float32)
    squares = jnp.sum(values * values, axis=1, keepdims=True)
    scaled = (values * norm_gain[None, :]).astype(jnp.bfloat16)

    def dot(a, b):
        return jnp.dot(a, b, preferred_element_type=jnp.float32)

    part_other = dot(scaled, w_in_other)
    part = jnp.concatenate(
        [dot(scaled, w_gate[0]), dot(scaled, w_up[0]), part_other], axis=1
    )
    total = part + lax.ppermute(part.astype(jnp.bfloat16), "xl", SWAP).astype(jnp.float32)
    squares = squares + lax.ppermute(squares, "xl", SWAP)
    total = total * lax.rsqrt(squares / D + EPSILON)
    total = total.reshape(rows, 2, 2, units)
    hidden = (jax.nn.silu(total[:, :, 0]) * total[:, :, 1]).astype(jnp.bfloat16)
    partial_value = dot(hidden[:, 0], w_down[0]) + dot(hidden[:, 1], w_down_other)
    returned = lax.all_to_all(
        partial_value.astype(jnp.bfloat16).reshape(depth, capacity, width),
        "z",
        split_axis=0,
        concat_axis=0,
        tiled=True,
    ).reshape(rows, width)

    wide = jnp.repeat(weight, spread, axis=1).T
    weighted = jnp.where(placed, jnp.repeat(wide, capacity, axis=0), 0.0)
    high = weighted.astype(jnp.bfloat16)
    low = (weighted - high.astype(jnp.float32)).astype(jnp.bfloat16)
    both = lax.dot_general(
        jnp.concatenate([high, low], axis=1),
        returned,
        (((0,), (0,)), ((), ())),
        preferred_element_type=jnp.float32,
    )
    return (both[:tokens] + both[tokens:]).astype(jnp.bfloat16)


def solution(mesh):
    x_hi = 2
    dp, expert, tensor = (mesh.shape[name] for name in ("dp", "expert", "tensor"))
    fine = Mesh(
        mesh.devices.reshape(dp // 2, 2, expert // x_hi, x_hi, tensor),
        ("y", "core", "z", "xh", "xl"),
    )
    tokens, slices = ("y", "core", "z", "xh"), ("z", "xh")
    return jax.shard_map(
        shards,
        mesh=fine,
        in_specs=(
            P(tokens, "xl"),
            P("xl"),
            P(tokens, None),
            P(tokens, None),
            P(slices, "xl", None),
            P(slices, "xl", None),
            P(slices, None, "xl"),
        ),
        out_specs=P(tokens, "xl"),
        check_vma=False,
    )
```

```python
import functools

import jax
import jax.numpy as jnp
from jax import lax
from jax.experimental import pallas as pl
from jax.experimental.pallas import tpu as pltpu
from jax.sharding import Mesh, PartitionSpec as P

D = 4096
EPSILON = 1e-06
SWAP = [(0, 1), (1, 0)]
PAIRS = [(i, i ^ 1) for i in range(16)]
LINES = [[0, 2, 4, 6, 9, 11, 13, 15], [1, 3, 5, 7, 8, 10, 12, 14]]
LANES = 128
VMEM_LIMIT = 16 * 1024 * 1024


def mm(a, b):
    return jnp.dot(a, b, preferred_element_type=jnp.float32)


def share_kernel(replica, gate_ref, up_ref, down_ref, near_ref, sems):
    _, depth, units = near_ref.shape
    rest = units - depth
    start = pl.multiple_of(replica[0] * depth, depth)
    rows = pl.ds(start, depth)
    pairs = [
        (gate_ref.at[rows], near_ref.at[0]),
        (up_ref.at[rows], near_ref.at[1]),
        (down_ref.at[pl.ds(0, depth), rows], near_ref.at[2, :, pl.ds(0, depth)]),
    ]
    for i in range(depth // rest):
        columns = pl.ds(pl.multiple_of(start + i * rest, rest), rest)
        pairs.append(
            (down_ref.at[pl.ds(depth, rest), columns], near_ref.at[2, pl.ds(i * rest, rest), pl.ds(depth, rest)])
        )
    copies = [pltpu.make_async_copy(a, b, sems.at[i]) for i, (a, b) in enumerate(pairs)]
    for copy in copies:
        copy.start()
    for copy in copies:
        copy.wait()


def share(replica, replicas, gate, up, down):
    width, units = gate.shape
    here = pl.BlockSpec(memory_space=pltpu.HBM)
    return pl.pallas_call(
        share_kernel,
        in_specs=[pl.BlockSpec(memory_space=pltpu.SMEM), here, here, here],
        out_specs=pl.BlockSpec(memory_space=pltpu.VMEM),
        out_shape=jax.ShapeDtypeStruct((3, width // replicas, units), gate.dtype),
        scratch_shapes=[pltpu.SemaphoreType.DMA((5,))],
        name="share",
    )(replica, gate, up, down)


def project_kernel(x_ref, gain_ref, gate_ref, up_ref, other_ref, send_ref):
    width, units = gate_ref.shape
    pieces = other_ref.shape[0]
    small = width // pieces
    values = x_ref[...].astype(jnp.float32)
    total = jnp.broadcast_to(jnp.sum(values * values, axis=1, keepdims=True), (values.shape[0], LANES))
    scaled = (values * gain_ref[...]).astype(jnp.bfloat16)
    for i, ref in enumerate((gate_ref, up_ref)):
        send_ref[:, i * units : (i + 1) * units] = mm(scaled, ref[...]).astype(jnp.bfloat16)
    for i in range(2):
        sums = mm(scaled[:, :small], other_ref[0, i])
        for piece in range(1, pieces):
            sums += mm(scaled[:, piece * small : (piece + 1) * small], other_ref[piece, i])
        send_ref[:, (2 + i) * units : (3 + i) * units] = sums.astype(jnp.bfloat16)
    high = total.astype(jnp.bfloat16).astype(jnp.float32)
    lane = lax.broadcasted_iota(jnp.int32, total.shape, 1)
    terms = jnp.where(lane == 0, high, jnp.where(lane == 1, total - high, 0.0))
    send_ref[:, 4 * units :] = terms.astype(jnp.bfloat16)


def project(rows, gain, gate, up, other):
    count, width = rows.shape
    units = gate.shape[1]
    near = pl.BlockSpec(memory_space=pltpu.VMEM)
    return pl.pallas_call(
        project_kernel,
        in_specs=[near] * 5,
        out_specs=near,
        out_shape=jax.ShapeDtypeStruct((count, 4 * units + LANES), jnp.bfloat16),
        compiler_params=pltpu.CompilerParams(vmem_limit_bytes=VMEM_LIMIT),
        cost_estimate=pl.CostEstimate(
            flops=8 * count * width * units, bytes_accessed=8 * width * units, transcendentals=0
        ),
        name="project",
    )(rows, gain, gate, up, other)


def expand_kernel(mine_ref, sent_ref, down_ref, other_ref, out_ref):
    units = down_ref.shape[0]

    def both(at, size):
        at = pl.ds(at, size)
        return mine_ref[:, at].astype(jnp.float32) + sent_ref[:, at].astype(jnp.float32)

    total = jnp.sum(both(4 * units, LANES), axis=1, keepdims=True)
    scale = lax.rsqrt(total / D + EPSILON)
    hidden = []
    for piece in range(2):
        gate, up = both(2 * units * piece, units), both(2 * units * piece + units, units)
        hidden.append((jax.nn.silu(gate * scale) * (up * scale)).astype(jnp.bfloat16))
    out = mm(hidden[0], down_ref[...])
    replicas, _, depth, _ = other_ref.shape
    rest = units - depth
    for i in range(replicas):
        part = mm(hidden[1][:, :depth], other_ref[i, 2, :, :depth])
        tail = [mm(hidden[1][:, depth:], other_ref[i, 2, j : j + rest, depth:]) for j in range(0, depth, rest)]
        at = slice(i * depth, (i + 1) * depth)
        out_ref[:, at] = (out[:, at] + part + jnp.concatenate(tail, axis=1)).astype(out_ref.dtype)


def expand(mine, sent, down, other, kind):
    count, (units, width) = mine.shape[0], down.shape
    near = pl.BlockSpec(memory_space=pltpu.VMEM)
    return pl.pallas_call(
        expand_kernel,
        in_specs=[near] * 4,
        out_specs=near,
        out_shape=jax.ShapeDtypeStruct((count, width), kind),
        compiler_params=pltpu.CompilerParams(vmem_limit_bytes=VMEM_LIMIT),
        cost_estimate=pl.CostEstimate(
            flops=4 * count * width * units, bytes_accessed=4 * width * units, transcendentals=count * units
        ),
        name="expand",
    )(mine, sent, down, other)


def shards(states, norm_gain, expert_ids, route_gates, w_gate, w_up, w_down):
    tokens, width = states.shape
    experts = lax.axis_size("z") // 2
    replicas = lax.axis_size("y") * lax.axis_size("core")
    capacity = tokens // 2
    rows = experts * capacity

    replica = lax.axis_index("y") * lax.axis_size("core") + lax.axis_index("core")
    near = share(replica.astype(jnp.int32)[None], replicas, w_gate[0], w_up[0], w_down[0])
    near = lax.ppermute(near, "xh", SWAP)

    flight_ids = jnp.arange(experts, dtype=jnp.int32)
    matches = expert_ids[:, :, None] == flight_ids[None, None, :]
    member = jnp.any(matches, axis=1)
    weight = jnp.sum(jnp.where(matches, route_gates[:, :, None], 0.0), axis=1)
    before = jnp.tril(jnp.ones((tokens, tokens), jnp.float32), -1)
    position = jnp.dot(before, member.astype(jnp.float32)).astype(jnp.int32)
    slots = jnp.where(member, position, capacity)
    slot_ids = jnp.arange(capacity, dtype=jnp.int32)
    placed = slots.T[:, None, :] == slot_ids[None, :, None]
    placed = placed.reshape(rows, tokens)
    packed = mm(placed.astype(jnp.bfloat16), states).astype(jnp.bfloat16)
    near, _ = lax.optimization_barrier((near, packed))
    other = lax.all_gather(near, ("y", "core"), axis=0)
    exchange = functools.partial(
        lax.all_to_all, axis_name="z", split_axis=0, concat_axis=0, axis_index_groups=LINES, tiled=True
    )
    first = exchange(packed.reshape(experts, capacity, width)).reshape(rows, width)
    second = lax.ppermute(first, "z", PAIRS)

    inputs = (norm_gain[None, :], w_gate[0], w_up[0], other)
    send1 = project(first, *inputs)
    send1, second = lax.optimization_barrier((send1, second))
    send2 = project(second, *inputs)
    sent2 = lax.ppermute(send2, "xl", SWAP)
    send1, _ = lax.optimization_barrier((send1, send2))
    sent1 = lax.ppermute(send1, "xl", SWAP)
    out2 = expand(send2, sent2, w_down[0], other, jnp.bfloat16)
    out1 = expand(send1, sent1, w_down[0], other, jnp.float32)
    out = (out1 + lax.ppermute(out2, "z", PAIRS).astype(jnp.float32)).astype(jnp.bfloat16)
    returned = exchange(out.reshape(experts, capacity, width)).reshape(rows, width)

    weighted = jnp.where(placed, jnp.repeat(weight.T, capacity, axis=0), 0.0)
    high = weighted.astype(jnp.bfloat16)
    low = (weighted - high.astype(jnp.float32)).astype(jnp.bfloat16)
    both = lax.dot_general(
        jnp.concatenate([high, low], axis=1),
        returned,
        (((0,), (0,)), ((), ())),
        preferred_element_type=jnp.float32,
    )
    return (both[:tokens] + both[tokens:]).astype(jnp.bfloat16)


def solution(mesh):
    dp, expert, tensor = (mesh.shape[name] for name in ("dp", "expert", "tensor"))
    fine = Mesh(
        mesh.devices.reshape(dp // 2, 2, expert // 2, 2, tensor),
        ("y", "core", "z", "xh", "xl"),
    )
    tokens, slices = ("y", "core", "z", "xh"), ("z", "xh")
    return jax.shard_map(
        shards,
        mesh=fine,
        in_specs=(
            P(tokens, "xl"),
            P("xl"),
            P(tokens, None),
            P(tokens, None),
            P(slices, "xl", None),
            P(slices, "xl", None),
            P(slices, None, "xl"),
        ),
        out_specs=P(tokens, "xl"),
        check_vma=False,
    )
```

```python
import functools

import jax
import jax.numpy as jnp
from jax import lax
from jax.experimental import pallas as pl
from jax.experimental.pallas import tpu as pltpu
from jax.sharding import Mesh, PartitionSpec as P

D = 4096
EPSILON = 1e-06
SWAP = [(0, 1), (1, 0)]
PAIRS = [(i, i ^ 1) for i in range(16)]
LINES = [[0, 2, 4, 6, 9, 11, 13, 15], [1, 3, 5, 7, 8, 10, 12, 14]]
LANES = 128
VMEM_LIMIT = 52 * 1024 * 1024
EXPAND_FLOPS = 402653184
WAIT_FLOPS = 1107000000
SCALE_FLOPS = 70848000000


def mm(a, b):
    return jnp.dot(a, b, preferred_element_type=jnp.float32)


def share_kernel(replica, gate_ref, up_ref, down_ref, near_ref, sems):
    _, depth, units = near_ref.shape
    rest = units - depth
    start = pl.multiple_of(replica[0] * depth, depth)
    rows = pl.ds(start, depth)
    pairs = [
        (gate_ref.at[rows], near_ref.at[0]),
        (up_ref.at[rows], near_ref.at[1]),
        (down_ref.at[pl.ds(0, depth), rows], near_ref.at[2, :, pl.ds(0, depth)]),
    ]
    for i in range(depth // rest):
        columns = pl.ds(pl.multiple_of(start + i * rest, rest), rest)
        pairs.append(
            (down_ref.at[pl.ds(depth, rest), columns], near_ref.at[2, pl.ds(i * rest, rest), pl.ds(depth, rest)])
        )
    copies = [pltpu.make_async_copy(a, b, sems.at[i]) for i, (a, b) in enumerate(pairs)]
    for copy in copies:
        copy.start()
    for copy in copies:
        copy.wait()


def share(replica, replicas, gate, up, down):
    width, units = gate.shape
    here = pl.BlockSpec(memory_space=pltpu.HBM)
    return pl.pallas_call(
        share_kernel,
        in_specs=[pl.BlockSpec(memory_space=pltpu.SMEM), here, here, here],
        out_specs=pl.BlockSpec(memory_space=pltpu.VMEM),
        out_shape=jax.ShapeDtypeStruct((3, width // replicas, units), gate.dtype),
        scratch_shapes=[pltpu.SemaphoreType.DMA((5,))],
        compiler_params=pltpu.CompilerParams(vmem_limit_bytes=VMEM_LIMIT),
        name="share",
    )(replica, gate, up, down)


def squares(values):
    total = jnp.broadcast_to(jnp.sum(values * values, axis=1, keepdims=True), (values.shape[0], LANES))
    high = total.astype(jnp.bfloat16).astype(jnp.float32)
    lane = lax.broadcasted_iota(jnp.int32, total.shape, 1)
    return jnp.where(lane == 0, high, jnp.where(lane == 1, total - high, 0.0)).astype(jnp.bfloat16)


def near_kernel(x_ref, gain_ref, gate_ref, up_ref, scaled_ref, send_ref, weights, sems):
    width, units = gate_ref.shape
    half = width // 2
    copies = []
    for step in range(2):
        rows = pl.ds(step * half, half)
        for i, ref in enumerate((gate_ref, up_ref)):
            copies.append(pltpu.make_async_copy(ref.at[rows], weights.at[i, rows], sems.at[step, i]))
            copies[-1].start()
    values = x_ref[...].astype(jnp.float32)
    send_ref[:, 2 * units :] = squares(values)
    scaled_ref[...] = (values * gain_ref[...]).astype(jnp.bfloat16)
    copies[0].wait()
    copies[1].wait()
    totals = [mm(scaled_ref[:, :half], weights[i, :half]) for i in range(2)]
    copies[2].wait()
    copies[3].wait()
    for i in range(2):
        total = totals[i] + mm(scaled_ref[:, half:], weights[i, half:])
        send_ref[:, i * units : (i + 1) * units] = total.astype(jnp.bfloat16)


def project_near(rows, gain, gate, up, flops):
    (count, width), units = rows.shape, gate.shape[1]
    near, here = pl.BlockSpec(memory_space=pltpu.VMEM), pl.BlockSpec(memory_space=pltpu.HBM)
    return pl.pallas_call(
        near_kernel,
        in_specs=[near] * 2 + [here] * 2,
        out_specs=[near] * 2,
        out_shape=[
            jax.ShapeDtypeStruct((count, width), jnp.bfloat16),
            jax.ShapeDtypeStruct((count, 2 * units + LANES), jnp.bfloat16),
        ],
        scratch_shapes=[pltpu.VMEM((2, width, units), jnp.bfloat16), pltpu.SemaphoreType.DMA((2, 2))],
        compiler_params=pltpu.CompilerParams(vmem_limit_bytes=VMEM_LIMIT),
        cost_estimate=pl.CostEstimate(flops=flops, bytes_accessed=4 * width * units, transcendentals=0),
        name="project_near",
    )(rows, gain, gate, up)


def far_kernel(scaled_ref, near_ref, other_ref, send_ref, weights, sems):
    pieces, _, depth, units = other_ref.shape
    half, copies = pieces // 2, []
    for piece in range(pieces):
        for i in range(2):
            rows = pl.ds(piece * depth, depth)
            copies.append(pltpu.make_async_copy(other_ref.at[piece, i], weights.at[i, rows], sems.at[piece, i]))
            copies[-1].start()
    kept = near_ref.shape[1]
    send_ref[:, :kept] = near_ref[...]
    totals = [None] * 2
    for step in range(2):
        for copy in copies[step * pieces : (step + 1) * pieces]:
            copy.wait()
        rows = slice(step * half * depth, (step + 1) * half * depth)
        for i in range(2):
            product = mm(scaled_ref[:, rows], weights[i, rows])
            totals[i] = product if step == 0 else totals[i] + product
    for i in range(2):
        send_ref[:, kept + i * units : kept + (i + 1) * units] = totals[i].astype(jnp.bfloat16)


def project_far(scaled, near_send, other):
    (count, width), (pieces, _, _, units) = scaled.shape, other.shape
    near, here = pl.BlockSpec(memory_space=pltpu.VMEM), pl.BlockSpec(memory_space=pltpu.HBM)
    return pl.pallas_call(
        far_kernel,
        in_specs=[near] * 2 + [here],
        out_specs=near,
        out_shape=jax.ShapeDtypeStruct((count, near_send.shape[1] + 2 * units), jnp.bfloat16),
        scratch_shapes=[pltpu.VMEM((2, width, units), jnp.bfloat16), pltpu.SemaphoreType.DMA((pieces, 2))],
        compiler_params=pltpu.CompilerParams(vmem_limit_bytes=VMEM_LIMIT),
        cost_estimate=pl.CostEstimate(
            flops=4 * count * width * units, bytes_accessed=4 * width * units, transcendentals=0
        ),
        name="project_far",
    )(scaled, near_send, other)


def expand_kernel(mine_ref, sent_ref, down_ref, other_ref, out_ref, down, hidden_ref, sems):
    units, width = down_ref.shape
    replicas, _, depth, _ = other_ref.shape
    rest = units - depth
    pairs = [(down_ref, down.at[pl.ds(0, units)])]
    for i in range(replicas):
        pairs.append(
            (other_ref.at[i, 2, :, pl.ds(0, depth)], down.at[pl.ds(units, depth), pl.ds(i * depth, depth)])
        )
        for j in range(0, depth, rest):
            pairs.append(
                (
                    other_ref.at[i, 2, pl.ds(j, rest), pl.ds(depth, rest)],
                    down.at[pl.ds(units + depth, rest), pl.ds(i * depth + j, rest)],
                )
            )
    copies = [pltpu.make_async_copy(a, b, sems.at[i]) for i, (a, b) in enumerate(pairs)]
    for copy in copies:
        copy.start()

    def both(at, size):
        at = pl.ds(at, size)
        return mine_ref[:, at].astype(jnp.float32) + sent_ref[:, at].astype(jnp.float32)

    total = jnp.sum(both(2 * units, LANES), axis=1, keepdims=True)
    scale = lax.rsqrt(total / D + EPSILON)
    for piece in range(2):
        at = piece * (2 * units + LANES)
        gate, up = both(at, units), both(at + units, units)
        hidden = jax.nn.silu(gate * scale) * (up * scale)
        hidden_ref[:, units * piece : units * (piece + 1)] = hidden.astype(jnp.bfloat16)
    for copy in copies:
        copy.wait()
    out_ref[...] = mm(hidden_ref[...], down[...]).astype(out_ref.dtype)


def expand(mine, sent, down, other, kind, flops):
    count, (units, width) = mine.shape[0], down.shape
    near, here = pl.BlockSpec(memory_space=pltpu.VMEM), pl.BlockSpec(memory_space=pltpu.HBM)
    replicas, _, depth, _ = other.shape
    return pl.pallas_call(
        expand_kernel,
        in_specs=[near] * 2 + [here] * 2,
        out_specs=near,
        out_shape=jax.ShapeDtypeStruct((count, width), kind),
        scratch_shapes=[
            pltpu.VMEM((2 * units, width), jnp.bfloat16),
            pltpu.VMEM((count, 2 * units), jnp.bfloat16),
            pltpu.SemaphoreType.DMA((1 + replicas * (1 + depth // (units - depth)),)),
        ],
        compiler_params=pltpu.CompilerParams(vmem_limit_bytes=VMEM_LIMIT),
        cost_estimate=pl.CostEstimate(
            flops=flops, bytes_accessed=4 * width * units, transcendentals=count * units
        ),
        name="expand",
    )(mine, sent, down, other)


def shards(states, norm_gain, expert_ids, route_gates, w_gate, w_up, w_down):
    tokens, width = states.shape
    experts = lax.axis_size("z") // 2
    replicas = lax.axis_size("y") * lax.axis_size("core")
    capacity = tokens // 2
    rows = experts * capacity

    replica = lax.axis_index("y") * lax.axis_size("core") + lax.axis_index("core")
    near = share(replica.astype(jnp.int32)[None], replicas, w_gate[0], w_up[0], w_down[0])
    near = lax.ppermute(near, "xh", SWAP)

    flight_ids = jnp.arange(experts, dtype=jnp.int32)
    matches = expert_ids[:, :, None] == flight_ids[None, None, :]
    member = jnp.any(matches, axis=1)
    weight = jnp.sum(jnp.where(matches, route_gates[:, :, None], 0.0), axis=1)
    before = jnp.tril(jnp.ones((tokens, tokens), jnp.float32), -1)
    position = jnp.dot(before, member.astype(jnp.float32)).astype(jnp.int32)
    slots = jnp.where(member, position, capacity)
    slot_ids = jnp.arange(capacity, dtype=jnp.int32)
    placed = slots.T[:, None, :] == slot_ids[None, :, None]
    placed = placed.reshape(rows, tokens)
    packed = mm(placed.astype(jnp.bfloat16), states).astype(jnp.bfloat16)
    near, _ = lax.optimization_barrier((near, packed))
    other = lax.all_gather(near, ("y", "core"), axis=0)
    exchange = functools.partial(
        lax.all_to_all, axis_name="z", split_axis=0, concat_axis=0, axis_index_groups=LINES, tiled=True
    )
    first = exchange(packed.reshape(experts, capacity, width)).reshape(rows, width)
    second = lax.ppermute(first, "z", PAIRS)

    gain = norm_gain[None, :]
    gate, up = w_gate[0], w_up[0]
    scaled1, near1 = project_near(first, gain, gate, up, SCALE_FLOPS)
    near1, second = lax.optimization_barrier((near1, second))
    scaled2, near2 = project_near(second, gain, gate, up, EXPAND_FLOPS)
    send2 = project_far(scaled2, near2, other)
    sent2 = lax.ppermute(send2, "xl", SWAP)
    near1, _ = lax.optimization_barrier((near1, send2))
    send1 = project_far(scaled1, near1, other)
    sent1 = lax.ppermute(send1, "xl", SWAP)
    out2 = expand(send2, sent2, w_down[0], other, jnp.bfloat16, EXPAND_FLOPS)
    out1 = expand(send1, sent1, w_down[0], other, jnp.float32, WAIT_FLOPS)
    out = (out1 + lax.ppermute(out2, "z", PAIRS).astype(jnp.float32)).astype(jnp.bfloat16)
    returned = exchange(out.reshape(experts, capacity, width)).reshape(rows, width)

    weighted = jnp.where(placed, jnp.repeat(weight.T, capacity, axis=0), 0.0)
    high = weighted.astype(jnp.bfloat16)
    low = (weighted - high.astype(jnp.float32)).astype(jnp.bfloat16)
    both = lax.dot_general(
        jnp.concatenate([high, low], axis=1),
        returned,
        (((0,), (0,)), ((), ())),
        preferred_element_type=jnp.float32,
    )
    return (both[:tokens] + both[tokens:]).astype(jnp.bfloat16)


def solution(mesh):
    dp, expert, tensor = (mesh.shape[name] for name in ("dp", "expert", "tensor"))
    fine = Mesh(
        mesh.devices.reshape(dp // 2, 2, expert // 2, 2, tensor),
        ("y", "core", "z", "xh", "xl"),
    )
    tokens, slices = ("y", "core", "z", "xh"), ("z", "xh")
    return jax.shard_map(
        shards,
        mesh=fine,
        in_specs=(
            P(tokens, "xl"),
            P("xl"),
            P(tokens, None),
            P(tokens, None),
            P(slices, "xl", None),
            P(slices, "xl", None),
            P(slices, None, "xl"),
        ),
        out_specs=P(tokens, "xl"),
        check_vma=False,
    )
```

```python
import functools

import jax
import jax.numpy as jnp
from jax import lax
from jax.experimental import pallas as pl
from jax.experimental.pallas import tpu as pltpu
from jax.sharding import Mesh, PartitionSpec as P

D = 4096
EPSILON = 1e-06
SWAP = [(0, 1), (1, 0)]
PAIRS = [(i, i ^ 1) for i in range(16)]
LINES = [[0, 2, 4, 6, 9, 11, 13, 15], [1, 3, 5, 7, 8, 10, 12, 14]]
LANES = 128
VMEM_LIMIT = 52 * 1024 * 1024
EXPAND_FLOPS = 402653184
WAIT_FLOPS = 1107000000
SCALE_FLOPS = 70848000000


def mm(a, b):
    return jnp.dot(a, b, preferred_element_type=jnp.float32)


def share_kernel(replica, gate_ref, up_ref, down_ref, near_ref, sems):
    _, depth, units = near_ref.shape
    rest = units - depth
    start = pl.multiple_of(replica[0] * depth, depth)
    rows = pl.ds(start, depth)
    pairs = [
        (gate_ref.at[rows], near_ref.at[0]),
        (up_ref.at[rows], near_ref.at[1]),
        (down_ref.at[pl.ds(0, depth), rows], near_ref.at[2, :, pl.ds(0, depth)]),
    ]
    for i in range(depth // rest):
        columns = pl.ds(pl.multiple_of(start + i * rest, rest), rest)
        pairs.append(
            (down_ref.at[pl.ds(depth, rest), columns], near_ref.at[2, pl.ds(i * rest, rest), pl.ds(depth, rest)])
        )
    copies = [pltpu.make_async_copy(a, b, sems.at[i]) for i, (a, b) in enumerate(pairs)]
    for copy in copies:
        copy.start()
    for copy in copies:
        copy.wait()


def share(replica, replicas, gate, up, down):
    width, units = gate.shape
    here = pl.BlockSpec(memory_space=pltpu.HBM)
    return pl.pallas_call(
        share_kernel,
        in_specs=[pl.BlockSpec(memory_space=pltpu.SMEM), here, here, here],
        out_specs=pl.BlockSpec(memory_space=pltpu.VMEM),
        out_shape=jax.ShapeDtypeStruct((3, width // replicas, units), gate.dtype),
        scratch_shapes=[pltpu.SemaphoreType.DMA((5,))],
        compiler_params=pltpu.CompilerParams(vmem_limit_bytes=VMEM_LIMIT),
        name="share",
    )(replica, gate, up, down)


def squares(values):
    total = jnp.broadcast_to(jnp.sum(values * values, axis=1, keepdims=True), (values.shape[0], LANES))
    high = total.astype(jnp.bfloat16).astype(jnp.float32)
    lane = lax.broadcasted_iota(jnp.int32, total.shape, 1)
    return jnp.where(lane == 0, high, jnp.where(lane == 1, total - high, 0.0)).astype(jnp.bfloat16)


def near_kernel(x_ref, gain_ref, gate_ref, up_ref, scaled_ref, send_ref, weights, sems):
    width, units = gate_ref.shape
    half = width // 2
    copies = []
    for step in range(2):
        rows = pl.ds(step * half, half)
        for i, ref in enumerate((gate_ref, up_ref)):
            copies.append(pltpu.make_async_copy(ref.at[rows], weights.at[i, rows], sems.at[step, i]))
            copies[-1].start()
    values = x_ref[...].astype(jnp.float32)
    send_ref[:, 2 * units :] = squares(values)
    scaled_ref[...] = (values * gain_ref[...]).astype(jnp.bfloat16)
    copies[0].wait()
    copies[1].wait()
    totals = [mm(scaled_ref[:, :half], weights[i, :half]) for i in range(2)]
    copies[2].wait()
    copies[3].wait()
    for i in range(2):
        total = totals[i] + mm(scaled_ref[:, half:], weights[i, half:])
        send_ref[:, i * units : (i + 1) * units] = total.astype(jnp.bfloat16)


def project_near(rows, gain, gate, up, flops):
    (count, width), units = rows.shape, gate.shape[1]
    near, here = pl.BlockSpec(memory_space=pltpu.VMEM), pl.BlockSpec(memory_space=pltpu.HBM)
    return pl.pallas_call(
        near_kernel,
        in_specs=[near] * 2 + [here] * 2,
        out_specs=[near] * 2,
        out_shape=[
            jax.ShapeDtypeStruct((count, width), jnp.bfloat16),
            jax.ShapeDtypeStruct((count, 2 * units + LANES), jnp.bfloat16),
        ],
        scratch_shapes=[pltpu.VMEM((2, width, units), jnp.bfloat16), pltpu.SemaphoreType.DMA((2, 2))],
        compiler_params=pltpu.CompilerParams(vmem_limit_bytes=VMEM_LIMIT),
        cost_estimate=pl.CostEstimate(flops=flops, bytes_accessed=4 * width * units, transcendentals=0),
        name="project_near",
    )(rows, gain, gate, up)


def far_kernel(first_ref, second_ref, near_ref, other_ref, first_send, early_send, late_send, weights, sems):
    pieces, _, depth, units = other_ref.shape
    count, kept = near_ref.shape
    half, part = pieces // 2, early_send.shape[0]
    copies = []
    for piece in range(pieces):
        for i in range(2):
            rows = pl.ds(piece * depth, depth)
            copies.append(pltpu.make_async_copy(other_ref.at[piece, i], weights.at[i, rows], sems.at[piece, i]))
            copies[-1].start()
    early_send[:, :kept] = near_ref[:part]
    late_send[:, :kept] = near_ref[part:]
    totals = [None] * 2
    for step in range(2):
        for copy in copies[step * pieces : (step + 1) * pieces]:
            copy.wait()
        rows = slice(step * half * depth, (step + 1) * half * depth)
        both = jnp.concatenate([second_ref[:, rows], first_ref[:, rows]])
        for i in range(2):
            product = mm(both, weights[i, rows])
            totals[i] = product if step == 0 else totals[i] + product
    for i in range(2):
        total = totals[i].astype(jnp.bfloat16)
        at = slice(kept + i * units, kept + (i + 1) * units)
        early_send[:, at] = total[:part]
        late_send[:, at] = total[part:count]
        first_send[:, i * units : (i + 1) * units] = total[count:]


def project_far(first, second, near_send, other):
    (count, width), (pieces, _, _, units) = first.shape, other.shape
    near, here = pl.BlockSpec(memory_space=pltpu.VMEM), pl.BlockSpec(memory_space=pltpu.HBM)
    shape = (count // 2, near_send.shape[1] + 2 * units)
    return pl.pallas_call(
        far_kernel,
        in_specs=[near] * 3 + [here],
        out_specs=[near] * 3,
        out_shape=[jax.ShapeDtypeStruct((count, 2 * units), jnp.bfloat16)]
        + [jax.ShapeDtypeStruct(shape, jnp.bfloat16)] * 2,
        scratch_shapes=[pltpu.VMEM((2, width, units), jnp.bfloat16), pltpu.SemaphoreType.DMA((pieces, 2))],
        compiler_params=pltpu.CompilerParams(vmem_limit_bytes=VMEM_LIMIT),
        cost_estimate=pl.CostEstimate(
            flops=8 * count * width * units, bytes_accessed=4 * width * units, transcendentals=0
        ),
        name="project_far",
    )(first, second, near_send, other)


def expand_kernel(near_ref, near_sent_ref, far_ref, far_sent_ref, down_ref, other_ref, out_ref, down, hidden_ref, sems):
    units = down_ref.shape[0]
    replicas, _, depth, _ = other_ref.shape
    rest = units - depth
    pairs = [(down_ref, down.at[pl.ds(0, units)])]
    for i in range(replicas):
        pairs.append(
            (other_ref.at[i, 2, :, pl.ds(0, depth)], down.at[pl.ds(units, depth), pl.ds(i * depth, depth)])
        )
        for j in range(0, depth, rest):
            pairs.append(
                (
                    other_ref.at[i, 2, pl.ds(j, rest), pl.ds(depth, rest)],
                    down.at[pl.ds(units + depth, rest), pl.ds(i * depth + j, rest)],
                )
            )
    copies = [pltpu.make_async_copy(a, b, sems.at[i]) for i, (a, b) in enumerate(pairs)]
    for copy in copies:
        copy.start()

    def both(mine, sent, at, size):
        at = pl.ds(at, size)
        return mine[:, at].astype(jnp.float32) + sent[:, at].astype(jnp.float32)

    total = jnp.sum(both(near_ref, near_sent_ref, 2 * units, LANES), axis=1, keepdims=True)
    scale = lax.rsqrt(total / D + EPSILON)
    kept = far_ref.shape[1] - 2 * units
    for piece, (mine, sent, at) in enumerate(((near_ref, near_sent_ref, 0), (far_ref, far_sent_ref, kept))):
        gate, up = both(mine, sent, at, units), both(mine, sent, at + units, units)
        hidden = jax.nn.silu(gate * scale) * (up * scale)
        hidden_ref[:, units * piece : units * (piece + 1)] = hidden.astype(jnp.bfloat16)
    copies[0].wait()
    out = mm(hidden_ref[:, :units], down[:units])
    for copy in copies[1:]:
        copy.wait()
    out_ref[...] = (out + mm(hidden_ref[:, units:], down[units:])).astype(out_ref.dtype)


def expand(near, near_sent, far, far_sent, down, other, kind, flops):
    count, (units, width) = near.shape[0], down.shape
    vmem, here = pl.BlockSpec(memory_space=pltpu.VMEM), pl.BlockSpec(memory_space=pltpu.HBM)
    replicas, _, depth, _ = other.shape
    return pl.pallas_call(
        expand_kernel,
        in_specs=[vmem] * 4 + [here] * 2,
        out_specs=vmem,
        out_shape=jax.ShapeDtypeStruct((count, width), kind),
        scratch_shapes=[
            pltpu.VMEM((2 * units, width), jnp.bfloat16),
            pltpu.VMEM((count, 2 * units), jnp.bfloat16),
            pltpu.SemaphoreType.DMA((1 + replicas * (1 + depth // (units - depth)),)),
        ],
        compiler_params=pltpu.CompilerParams(vmem_limit_bytes=VMEM_LIMIT),
        cost_estimate=pl.CostEstimate(
            flops=flops, bytes_accessed=4 * width * units, transcendentals=count * units
        ),
        name="expand",
    )(near, near_sent, far, far_sent, down, other)


def shards(states, norm_gain, expert_ids, route_gates, w_gate, w_up, w_down):
    tokens, width = states.shape
    experts = lax.axis_size("z") // 2
    replicas = lax.axis_size("y") * lax.axis_size("core")
    capacity = tokens // 2
    rows = experts * capacity

    replica = lax.axis_index("y") * lax.axis_size("core") + lax.axis_index("core")
    near = share(replica.astype(jnp.int32)[None], replicas, w_gate[0], w_up[0], w_down[0])
    near = lax.ppermute(near, "xh", SWAP)

    flight_ids = jnp.arange(experts, dtype=jnp.int32)
    matches = expert_ids[:, :, None] == flight_ids[None, None, :]
    member = jnp.any(matches, axis=1)
    weight = jnp.sum(jnp.where(matches, route_gates[:, :, None], 0.0), axis=1)
    before = jnp.tril(jnp.ones((tokens, tokens), jnp.float32), -1)
    position = jnp.dot(before, member.astype(jnp.float32)).astype(jnp.int32)
    slots = jnp.where(member, position, capacity)
    slot_ids = jnp.arange(capacity, dtype=jnp.int32)
    placed = slots.T[:, None, :] == slot_ids[None, :, None]
    placed = placed.reshape(rows, tokens)
    packed = mm(placed.astype(jnp.bfloat16), states).astype(jnp.bfloat16)
    near, _ = lax.optimization_barrier((near, packed))
    other = lax.all_gather(near, ("y", "core"), axis=0)
    exchange = functools.partial(
        lax.all_to_all, axis_name="z", split_axis=0, concat_axis=0, axis_index_groups=LINES, tiled=True
    )
    first = exchange(packed.reshape(experts, capacity, width)).reshape(rows, width)
    second = lax.ppermute(first, "z", PAIRS)

    gain = norm_gain[None, :]
    gate, up = w_gate[0], w_up[0]
    scaled1, near1 = project_near(first, gain, gate, up, SCALE_FLOPS)
    near_sent1 = lax.ppermute(near1, "xl", SWAP)
    near_sent1, second = lax.optimization_barrier((near_sent1, second))
    scaled2, near2 = project_near(second, gain, gate, up, EXPAND_FLOPS)
    far1, early, late = project_far(scaled1, scaled2, near2, other)
    early_sent = lax.ppermute(early, "xl", SWAP)
    late_sent = lax.ppermute(late, "xl", SWAP)
    far_sent1 = lax.ppermute(far1, "xl", SWAP)
    down = w_down[0]
    outs = [expand(early, early_sent, early, early_sent, down, other, jnp.bfloat16, EXPAND_FLOPS)]
    outs.append(expand(late, late_sent, late, late_sent, down, other, jnp.bfloat16, EXPAND_FLOPS))
    out1 = expand(near1, near_sent1, far1, far_sent1, down, other, jnp.bfloat16, WAIT_FLOPS)
    back = jnp.concatenate([lax.ppermute(x, "z", PAIRS) for x in outs])
    out = (out1.astype(jnp.float32) + back.astype(jnp.float32)).astype(jnp.bfloat16)
    returned = exchange(out.reshape(experts, capacity, width)).reshape(rows, width)

    weighted = jnp.where(placed, jnp.repeat(weight.T, capacity, axis=0), 0.0)
    high = weighted.astype(jnp.bfloat16)
    low = (weighted - high.astype(jnp.float32)).astype(jnp.bfloat16)
    both = lax.dot_general(
        jnp.concatenate([high, low], axis=1),
        returned,
        (((0,), (0,)), ((), ())),
        preferred_element_type=jnp.float32,
    )
    return (both[:tokens] + both[tokens:]).astype(jnp.bfloat16)


def solution(mesh):
    dp, expert, tensor = (mesh.shape[name] for name in ("dp", "expert", "tensor"))
    fine = Mesh(
        mesh.devices.reshape(dp // 2, 2, expert // 2, 2, tensor),
        ("y", "core", "z", "xh", "xl"),
    )
    tokens, slices = ("y", "core", "z", "xh"), ("z", "xh")
    return jax.shard_map(
        shards,
        mesh=fine,
        in_specs=(
            P(tokens, "xl"),
            P("xl"),
            P(tokens, None),
            P(tokens, None),
            P(slices, "xl", None),
            P(slices, "xl", None),
            P(slices, None, "xl"),
        ),
        out_specs=P(tokens, "xl"),
        check_vma=False,
    )
```

```python
import functools

import jax
import jax.numpy as jnp
from jax import lax
from jax.experimental import pallas as pl
from jax.experimental.pallas import tpu as pltpu
from jax.sharding import Mesh, PartitionSpec as P

D = 4096
EPSILON = 1e-06
SWAP = [(0, 1), (1, 0)]
PAIRS = [(i, i ^ 1) for i in range(16)]
LINES = [[0, 2, 4, 6, 9, 11, 13, 15], [1, 3, 5, 7, 8, 10, 12, 14]]
LANES = 128
VMEM_LIMIT = 16 * 1024 * 1024
EXPAND_FLOPS = 402653184
WAIT_FLOPS = 1000000
SCALE_FLOPS = 70848000000


def mm(a, b):
    return jnp.dot(a, b, preferred_element_type=jnp.float32)


def hbm(*arrays):
    return [pltpu.with_memory_space_constraint(a, pltpu.HBM) for a in arrays]


def share_kernel(replica, gate_ref, up_ref, down_ref, near_ref, sems):
    _, depth, units = near_ref.shape
    rest = units - depth
    start = pl.multiple_of(replica[0] * depth, depth)
    rows = pl.ds(start, depth)
    pairs = [
        (gate_ref.at[rows], near_ref.at[0]),
        (up_ref.at[rows], near_ref.at[1]),
        (down_ref.at[pl.ds(0, depth), rows], near_ref.at[2, :, pl.ds(0, depth)]),
    ]
    for i in range(depth // rest):
        columns = pl.ds(pl.multiple_of(start + i * rest, rest), rest)
        pairs.append(
            (down_ref.at[pl.ds(depth, rest), columns], near_ref.at[2, pl.ds(i * rest, rest), pl.ds(depth, rest)])
        )
    copies = [pltpu.make_async_copy(a, b, sems.at[i]) for i, (a, b) in enumerate(pairs)]
    for copy in copies:
        copy.start()
    for copy in copies:
        copy.wait()


def share(replica, replicas, gate, up, down):
    width, units = gate.shape
    here = pl.BlockSpec(memory_space=pltpu.HBM)
    return pl.pallas_call(
        share_kernel,
        in_specs=[pl.BlockSpec(memory_space=pltpu.SMEM), here, here, here],
        out_specs=pl.BlockSpec(memory_space=pltpu.VMEM),
        out_shape=jax.ShapeDtypeStruct((3, width // replicas, units), gate.dtype),
        scratch_shapes=[pltpu.SemaphoreType.DMA((5,))],
        compiler_params=pltpu.CompilerParams(vmem_limit_bytes=VMEM_LIMIT),
        name="share",
    )(replica, *hbm(gate, up, down))


def squares(values):
    total = jnp.broadcast_to(jnp.sum(values * values, axis=1, keepdims=True), (values.shape[0], LANES))
    high = total.astype(jnp.bfloat16).astype(jnp.float32)
    lane = lax.broadcasted_iota(jnp.int32, total.shape, 1)
    return jnp.where(lane == 0, high, jnp.where(lane == 1, total - high, 0.0)).astype(jnp.bfloat16)


def near_kernel(x_ref, gain_ref, gate_ref, up_ref, scaled_ref, send_ref, weights, sems):
    width, units = gate_ref.shape
    half = width // 2
    copies = []
    for step in range(2):
        rows = pl.ds(step * half, half)
        for i, ref in enumerate((gate_ref, up_ref)):
            copies.append(pltpu.make_async_copy(ref.at[rows], weights.at[i, rows], sems.at[step, i]))
            copies[-1].start()
    values = x_ref[...].astype(jnp.float32)
    send_ref[:, 2 * units :] = squares(values)
    scaled_ref[...] = (values * gain_ref[...]).astype(jnp.bfloat16)
    copies[0].wait()
    copies[1].wait()
    totals = [mm(scaled_ref[:, :half], weights[i, :half]) for i in range(2)]
    copies[2].wait()
    copies[3].wait()
    for i in range(2):
        total = totals[i] + mm(scaled_ref[:, half:], weights[i, half:])
        send_ref[:, i * units : (i + 1) * units] = total.astype(jnp.bfloat16)


def project_near(rows, gain, gate, up, flops):
    (count, width), units = rows.shape, gate.shape[1]
    near, here = pl.BlockSpec(memory_space=pltpu.VMEM), pl.BlockSpec(memory_space=pltpu.HBM)
    return pl.pallas_call(
        near_kernel,
        in_specs=[near] * 2 + [here] * 2,
        out_specs=[near] * 3,
        out_shape=[
            jax.ShapeDtypeStruct((count, width), jnp.bfloat16),
            jax.ShapeDtypeStruct((count, 2 * units + LANES), jnp.bfloat16),
            pltpu.VMEM((2, width, units), jnp.bfloat16),
        ],
        scratch_shapes=[pltpu.SemaphoreType.DMA((2, 2))],
        compiler_params=pltpu.CompilerParams(vmem_limit_bytes=VMEM_LIMIT),
        cost_estimate=pl.CostEstimate(flops=flops, bytes_accessed=4 * width * units, transcendentals=0),
        name="project_near",
    )(rows, gain, *hbm(gate, up))


def again_kernel(x_ref, gain_ref, weights, scaled_ref, send_ref):
    units = weights.shape[2]
    values = x_ref[...].astype(jnp.float32)
    send_ref[:, 2 * units :] = squares(values)
    scaled_ref[...] = (values * gain_ref[...]).astype(jnp.bfloat16)
    for i in range(2):
        send_ref[:, i * units : (i + 1) * units] = mm(scaled_ref[...], weights[i]).astype(jnp.bfloat16)


def project_again(rows, gain, weights):
    (count, width), units = rows.shape, weights.shape[2]
    near = pl.BlockSpec(memory_space=pltpu.VMEM)
    return pl.pallas_call(
        again_kernel,
        in_specs=[near] * 3,
        out_specs=[near] * 2,
        out_shape=[
            jax.ShapeDtypeStruct((count, width), jnp.bfloat16),
            jax.ShapeDtypeStruct((count, 2 * units + LANES), jnp.bfloat16),
        ],
        compiler_params=pltpu.CompilerParams(vmem_limit_bytes=VMEM_LIMIT),
        cost_estimate=pl.CostEstimate(
            flops=4 * count * width * units, bytes_accessed=4 * width * units, transcendentals=0
        ),
        name="project_again",
    )(rows, gain, pltpu.with_memory_space_constraint(weights, pltpu.VMEM))


def far_kernel(first_ref, second_ref, near_ref, other_ref, first_send, early_send, late_send, weights, sems):
    pieces, _, depth, units = other_ref.shape
    count, kept = near_ref.shape
    half, part = pieces // 2, early_send.shape[0]
    copies = []
    for piece in range(pieces):
        for i in range(2):
            rows = pl.ds(piece * depth, depth)
            copies.append(pltpu.make_async_copy(other_ref.at[piece, i], weights.at[i, rows], sems.at[piece, i]))
            copies[-1].start()
    early_send[:, :kept] = near_ref[:part]
    late_send[:, :kept] = near_ref[part:]
    totals = [None] * 2
    for step in range(2):
        for copy in copies[step * pieces : (step + 1) * pieces]:
            copy.wait()
        rows = slice(step * half * depth, (step + 1) * half * depth)
        both = jnp.concatenate([second_ref[:, rows], first_ref[:, rows]])
        for i in range(2):
            product = mm(both, weights[i, rows])
            totals[i] = product if step == 0 else totals[i] + product
    for i in range(2):
        total = totals[i].astype(jnp.bfloat16)
        at = slice(kept + i * units, kept + (i + 1) * units)
        early_send[:, at] = total[:part]
        late_send[:, at] = total[part:count]
        first_send[:, i * units : (i + 1) * units] = total[count:]


def project_far(first, second, near_send, other):
    (count, width), (pieces, _, _, units) = first.shape, other.shape
    near, here = pl.BlockSpec(memory_space=pltpu.VMEM), pl.BlockSpec(memory_space=pltpu.HBM)
    shape = (count // 2, near_send.shape[1] + 2 * units)
    return pl.pallas_call(
        far_kernel,
        in_specs=[near] * 3 + [here],
        out_specs=[near] * 3,
        out_shape=[jax.ShapeDtypeStruct((count, 2 * units), jnp.bfloat16)]
        + [jax.ShapeDtypeStruct(shape, jnp.bfloat16)] * 2,
        scratch_shapes=[
            pltpu.VMEM((2, width, units), jnp.bfloat16),
            pltpu.SemaphoreType.DMA((pieces, 2)),
        ],
        compiler_params=pltpu.CompilerParams(vmem_limit_bytes=VMEM_LIMIT),
        cost_estimate=pl.CostEstimate(
            flops=8 * count * width * units, bytes_accessed=4 * width * units, transcendentals=0
        ),
        name="project_far",
    )(first, second, near_send, *hbm(other))


def stack_kernel(other_ref, down_ref, out_ref, sems):
    pieces, _, depth, units = other_ref.shape
    rest = units - depth
    pairs = [(down_ref, out_ref.at[pl.ds(0, units)])]
    for i in range(pieces):
        pairs.append(
            (other_ref.at[i, 2, :, pl.ds(0, depth)], out_ref.at[pl.ds(units, depth), pl.ds(i * depth, depth)])
        )
        for j in range(0, depth, rest):
            pairs.append(
                (
                    other_ref.at[i, 2, pl.ds(j, rest), pl.ds(depth, rest)],
                    out_ref.at[pl.ds(units + depth, rest), pl.ds(i * depth + j, rest)],
                )
            )
    copies = [pltpu.make_async_copy(a, b, sems.at[i]) for i, (a, b) in enumerate(pairs)]
    for copy in copies:
        copy.start()
    for copy in copies:
        copy.wait()


def stack(other, down):
    here = pl.BlockSpec(memory_space=pltpu.HBM)
    (pieces, _, depth, units), width = other.shape, down.shape[1]
    return pl.pallas_call(
        stack_kernel,
        in_specs=[here] * 2,
        out_specs=pl.BlockSpec(memory_space=pltpu.VMEM),
        out_shape=pltpu.VMEM((2 * units, width), jnp.bfloat16),
        scratch_shapes=[pltpu.SemaphoreType.DMA((1 + pieces * (1 + depth // (units - depth)),))],
        compiler_params=pltpu.CompilerParams(vmem_limit_bytes=VMEM_LIMIT),
        cost_estimate=pl.CostEstimate(flops=0, bytes_accessed=8 * units * width, transcendentals=0),
        name="stack",
    )(*hbm(other, down))


def expand_kernel(near_ref, near_sent_ref, far_ref, far_sent_ref, down_ref, out_ref, hidden_ref):
    units = down_ref.shape[0] // 2

    def both(mine, sent, at, size):
        at = pl.ds(at, size)
        return mine[:, at].astype(jnp.float32) + sent[:, at].astype(jnp.float32)

    total = jnp.sum(both(near_ref, near_sent_ref, 2 * units, LANES), axis=1, keepdims=True)
    scale = lax.rsqrt(total / D + EPSILON)
    kept = far_ref.shape[1] - 2 * units
    for piece, (mine, sent, at) in enumerate(((near_ref, near_sent_ref, 0), (far_ref, far_sent_ref, kept))):
        gate, up = both(mine, sent, at, units), both(mine, sent, at + units, units)
        hidden = jax.nn.silu(gate * scale) * (up * scale)
        hidden_ref[:, units * piece : units * (piece + 1)] = hidden.astype(jnp.bfloat16)
    out_ref[...] = mm(hidden_ref[...], down_ref[...]).astype(out_ref.dtype)


def expand(near, near_sent, far, far_sent, down, kind, flops):
    count, (units, width) = near.shape[0], down.shape
    vmem = pl.BlockSpec(memory_space=pltpu.VMEM)
    return pl.pallas_call(
        expand_kernel,
        in_specs=[vmem] * 5,
        out_specs=vmem,
        out_shape=jax.ShapeDtypeStruct((count, width), kind),
        scratch_shapes=[pltpu.VMEM((count, units), jnp.bfloat16)],
        compiler_params=pltpu.CompilerParams(vmem_limit_bytes=VMEM_LIMIT),
        cost_estimate=pl.CostEstimate(
            flops=flops, bytes_accessed=2 * width * units, transcendentals=count * units
        ),
        name="expand",
    )(near, near_sent, far, far_sent, pltpu.with_memory_space_constraint(down, pltpu.VMEM))


def shards(states, norm_gain, expert_ids, route_gates, w_gate, w_up, w_down):
    tokens, width = states.shape
    experts = lax.axis_size("z") // 2
    replicas = lax.axis_size("y") * lax.axis_size("core")
    capacity = tokens // 2
    rows = experts * capacity

    replica = lax.axis_index("y") * lax.axis_size("core") + lax.axis_index("core")
    near = share(replica.astype(jnp.int32)[None], replicas, w_gate[0], w_up[0], w_down[0])
    near = lax.ppermute(near, "xh", SWAP)

    flight_ids = jnp.arange(experts, dtype=jnp.int32)
    matches = expert_ids[:, :, None] == flight_ids[None, None, :]
    member = jnp.any(matches, axis=1)
    weight = jnp.sum(jnp.where(matches, route_gates[:, :, None], 0.0), axis=1)
    before = jnp.tril(jnp.ones((tokens, tokens), jnp.float32), -1)
    position = jnp.dot(before, member.astype(jnp.float32)).astype(jnp.int32)
    slots = jnp.where(member, position, capacity)
    slot_ids = jnp.arange(capacity, dtype=jnp.int32)
    placed = slots.T[:, None, :] == slot_ids[None, :, None]
    placed = placed.reshape(rows, tokens)
    packed = mm(placed.astype(jnp.bfloat16), states).astype(jnp.bfloat16)
    near, _ = lax.optimization_barrier((near, packed))
    other = lax.all_gather(near, ("y", "core"), axis=0)
    exchange = functools.partial(
        lax.all_to_all, axis_name="z", split_axis=0, concat_axis=0, axis_index_groups=LINES, tiled=True
    )
    first = exchange(packed.reshape(experts, capacity, width)).reshape(rows, width)
    second = lax.ppermute(first, "z", PAIRS)

    gain = norm_gain[None, :]
    gate, up = w_gate[0], w_up[0]
    scaled1, near1, weights = project_near(first, gain, gate, up, SCALE_FLOPS)
    near_sent1 = lax.ppermute(near1, "xl", SWAP)
    near_sent1, second = lax.optimization_barrier((near_sent1, second))
    scaled2, near2 = project_again(second, gain, weights)
    far1, early, late = project_far(scaled1, scaled2, near2, other)
    early_sent = lax.ppermute(early, "xl", SWAP)
    late_sent = lax.ppermute(late, "xl", SWAP)
    other, _ = lax.optimization_barrier((other, early))
    down = stack(other, w_down[0])
    outs = [expand(early, early_sent, early, early_sent, down, jnp.bfloat16, EXPAND_FLOPS)]
    far1, _ = lax.optimization_barrier((far1, outs[0]))
    far_sent1 = lax.ppermute(far1, "xl", SWAP)
    outs.append(expand(late, late_sent, late, late_sent, down, jnp.bfloat16, EXPAND_FLOPS))
    out1 = expand(near1, near_sent1, far1, far_sent1, down, jnp.bfloat16, WAIT_FLOPS)
    back = jnp.concatenate([lax.ppermute(x, "z", PAIRS) for x in outs])
    out = (out1.astype(jnp.float32) + back.astype(jnp.float32)).astype(jnp.bfloat16)
    returned = exchange(out.reshape(experts, capacity, width)).reshape(rows, width)

    weighted = jnp.where(placed, jnp.repeat(weight.T, capacity, axis=0), 0.0)
    high = weighted.astype(jnp.bfloat16)
    low = (weighted - high.astype(jnp.float32)).astype(jnp.bfloat16)
    both = lax.dot_general(
        jnp.concatenate([high, low], axis=1),
        returned,
        (((0,), (0,)), ((), ())),
        preferred_element_type=jnp.float32,
    )
    return (both[:tokens] + both[tokens:]).astype(jnp.bfloat16)


def solution(mesh):
    dp, expert, tensor = (mesh.shape[name] for name in ("dp", "expert", "tensor"))
    fine = Mesh(
        mesh.devices.reshape(dp // 2, 2, expert // 2, 2, tensor),
        ("y", "core", "z", "xh", "xl"),
    )
    tokens, slices = ("y", "core", "z", "xh"), ("z", "xh")
    return jax.shard_map(
        shards,
        mesh=fine,
        in_specs=(
            P(tokens, "xl"),
            P("xl"),
            P(tokens, None),
            P(tokens, None),
            P(slices, "xl", None),
            P(slices, "xl", None),
            P(slices, None, "xl"),
        ),
        out_specs=P(tokens, "xl"),
        check_vma=False,
    )
```

```python
import functools

import jax
import jax.numpy as jnp
from jax import lax
from jax.experimental import pallas as pl
from jax.experimental.pallas import tpu as pltpu
from jax.sharding import Mesh, PartitionSpec as P

D = 4096
EPSILON = 1e-06
SWAP = [(0, 1), (1, 0)]
PAIRS = [(i, i ^ 1) for i in range(16)]
LINES = [[0, 2, 4, 6, 9, 11, 13, 15], [1, 3, 5, 7, 8, 10, 12, 14]]
LANES = 128
VMEM_LIMIT = 16 * 1024 * 1024
EXPAND_FLOPS = 402653184
WAIT_FLOPS = 1000000
SCALE_FLOPS = 70848000000


def mm(a, b):
    return jnp.dot(a, b, preferred_element_type=jnp.float32)


def hbm(*arrays):
    return [pltpu.with_memory_space_constraint(a, pltpu.HBM) for a in arrays]


def share_kernel(replica, gate_ref, up_ref, down_ref, near_ref, sems):
    _, depth, units = near_ref.shape
    rest = units - depth
    start = pl.multiple_of(replica[0] * depth, depth)
    rows = pl.ds(start, depth)
    pairs = [
        (gate_ref.at[rows], near_ref.at[0]),
        (up_ref.at[rows], near_ref.at[1]),
        (down_ref.at[pl.ds(0, depth), rows], near_ref.at[2, :, pl.ds(0, depth)]),
    ]
    for i in range(depth // rest):
        columns = pl.ds(pl.multiple_of(start + i * rest, rest), rest)
        pairs.append(
            (down_ref.at[pl.ds(depth, rest), columns], near_ref.at[2, pl.ds(i * rest, rest), pl.ds(depth, rest)])
        )
    copies = [pltpu.make_async_copy(a, b, sems.at[i]) for i, (a, b) in enumerate(pairs)]
    for copy in copies:
        copy.start()
    for copy in copies:
        copy.wait()


def share(replica, replicas, gate, up, down):
    width, units = gate.shape
    here = pl.BlockSpec(memory_space=pltpu.HBM)
    return pl.pallas_call(
        share_kernel,
        in_specs=[pl.BlockSpec(memory_space=pltpu.SMEM), here, here, here],
        out_specs=pl.BlockSpec(memory_space=pltpu.VMEM),
        out_shape=jax.ShapeDtypeStruct((3, width // replicas, units), gate.dtype),
        scratch_shapes=[pltpu.SemaphoreType.DMA((5,))],
        compiler_params=pltpu.CompilerParams(vmem_limit_bytes=VMEM_LIMIT),
        name="share",
    )(replica, *hbm(gate, up, down))


def pack_kernel(placed_ref, states_ref, packed_ref):
    packed_ref[...] = mm(placed_ref[...], states_ref[...]).astype(packed_ref.dtype)


def pack(placed, states):
    near = pl.BlockSpec(memory_space=pltpu.VMEM)
    return pl.pallas_call(
        pack_kernel,
        in_specs=[near] * 2,
        out_specs=near,
        out_shape=pltpu.VMEM((placed.shape[0], states.shape[1]), jnp.bfloat16),
        compiler_params=pltpu.CompilerParams(vmem_limit_bytes=VMEM_LIMIT),
        cost_estimate=pl.CostEstimate(
            flops=2 * placed.size * states.shape[1], bytes_accessed=8 * states.size, transcendentals=0
        ),
        name="pack",
    )(placed, states)


def squares(values):
    total = jnp.broadcast_to(jnp.sum(values * values, axis=1, keepdims=True), (values.shape[0], LANES))
    high = total.astype(jnp.bfloat16).astype(jnp.float32)
    lane = lax.broadcasted_iota(jnp.int32, total.shape, 1)
    return jnp.where(lane == 0, high, jnp.where(lane == 1, total - high, 0.0)).astype(jnp.bfloat16)


def near_kernel(x_ref, gain_ref, gate_ref, up_ref, scaled_ref, send_ref, weights, sems):
    width, units = gate_ref.shape
    half = width // 2
    copies = []
    for step in range(2):
        rows = pl.ds(step * half, half)
        for i, ref in enumerate((gate_ref, up_ref)):
            copies.append(pltpu.make_async_copy(ref.at[rows], weights.at[i, rows], sems.at[step, i]))
            copies[-1].start()
    values = x_ref[...].astype(jnp.float32)
    send_ref[:, 2 * units :] = squares(values)
    scaled_ref[...] = (values * gain_ref[...]).astype(jnp.bfloat16)
    copies[0].wait()
    copies[1].wait()
    totals = [mm(scaled_ref[:, :half], weights[i, :half]) for i in range(2)]
    copies[2].wait()
    copies[3].wait()
    for i in range(2):
        total = totals[i] + mm(scaled_ref[:, half:], weights[i, half:])
        send_ref[:, i * units : (i + 1) * units] = total.astype(jnp.bfloat16)


def project_near(rows, gain, gate, up, flops):
    (count, width), units = rows.shape, gate.shape[1]
    near, here = pl.BlockSpec(memory_space=pltpu.VMEM), pl.BlockSpec(memory_space=pltpu.HBM)
    return pl.pallas_call(
        near_kernel,
        in_specs=[near] * 2 + [here] * 2,
        out_specs=[near] * 3,
        out_shape=[
            jax.ShapeDtypeStruct((count, width), jnp.bfloat16),
            jax.ShapeDtypeStruct((count, 2 * units + LANES), jnp.bfloat16),
            pltpu.VMEM((2, width, units), jnp.bfloat16),
        ],
        scratch_shapes=[pltpu.SemaphoreType.DMA((2, 2))],
        compiler_params=pltpu.CompilerParams(vmem_limit_bytes=VMEM_LIMIT),
        cost_estimate=pl.CostEstimate(flops=flops, bytes_accessed=4 * width * units, transcendentals=0),
        name="project_near",
    )(rows, gain, *hbm(gate, up))


def again_kernel(x_ref, gain_ref, weights, scaled_ref, send_ref):
    units = weights.shape[2]
    values = x_ref[...].astype(jnp.float32)
    send_ref[:, 2 * units :] = squares(values)
    scaled_ref[...] = (values * gain_ref[...]).astype(jnp.bfloat16)
    for i in range(2):
        send_ref[:, i * units : (i + 1) * units] = mm(scaled_ref[...], weights[i]).astype(jnp.bfloat16)


def project_again(rows, gain, weights):
    (count, width), units = rows.shape, weights.shape[2]
    near = pl.BlockSpec(memory_space=pltpu.VMEM)
    return pl.pallas_call(
        again_kernel,
        in_specs=[near] * 3,
        out_specs=[near] * 2,
        out_shape=[
            jax.ShapeDtypeStruct((count, width), jnp.bfloat16),
            jax.ShapeDtypeStruct((count, 2 * units + LANES), jnp.bfloat16),
        ],
        compiler_params=pltpu.CompilerParams(vmem_limit_bytes=VMEM_LIMIT),
        cost_estimate=pl.CostEstimate(
            flops=4 * count * width * units, bytes_accessed=4 * width * units, transcendentals=0
        ),
        name="project_again",
    )(rows, gain, pltpu.with_memory_space_constraint(weights, pltpu.VMEM))


def far_kernel(first_ref, second_ref, near_ref, other_ref, first_send, early_send, late_send, weights, sems):
    pieces, _, depth, units = other_ref.shape
    count, kept = near_ref.shape
    half, part = pieces // 2, early_send.shape[0]
    copies = []
    for piece in range(pieces):
        for i in range(2):
            rows = pl.ds(piece * depth, depth)
            copies.append(pltpu.make_async_copy(other_ref.at[piece, i], weights.at[i, rows], sems.at[piece, i]))
            copies[-1].start()
    early_send[:, :kept] = near_ref[:part]
    late_send[:, :kept] = near_ref[part:]
    totals = [None] * 2
    for step in range(2):
        for copy in copies[step * pieces : (step + 1) * pieces]:
            copy.wait()
        rows = slice(step * half * depth, (step + 1) * half * depth)
        both = jnp.concatenate([second_ref[:, rows], first_ref[:, rows]])
        for i in range(2):
            product = mm(both, weights[i, rows])
            totals[i] = product if step == 0 else totals[i] + product
    for i in range(2):
        total = totals[i].astype(jnp.bfloat16)
        at = slice(kept + i * units, kept + (i + 1) * units)
        early_send[:, at] = total[:part]
        late_send[:, at] = total[part:count]
        first_send[:, i * units : (i + 1) * units] = total[count:]


def project_far(first, second, near_send, other):
    (count, width), (pieces, _, _, units) = first.shape, other.shape
    near, here = pl.BlockSpec(memory_space=pltpu.VMEM), pl.BlockSpec(memory_space=pltpu.HBM)
    shape = (count // 2, near_send.shape[1] + 2 * units)
    return pl.pallas_call(
        far_kernel,
        in_specs=[near] * 3 + [here],
        out_specs=[near] * 3,
        out_shape=[jax.ShapeDtypeStruct((count, 2 * units), jnp.bfloat16)]
        + [jax.ShapeDtypeStruct(shape, jnp.bfloat16)] * 2,
        scratch_shapes=[
            pltpu.VMEM((2, width, units), jnp.bfloat16),
            pltpu.SemaphoreType.DMA((pieces, 2)),
        ],
        compiler_params=pltpu.CompilerParams(vmem_limit_bytes=VMEM_LIMIT),
        cost_estimate=pl.CostEstimate(
            flops=8 * count * width * units, bytes_accessed=4 * width * units, transcendentals=0
        ),
        name="project_far",
    )(first, second, near_send, *hbm(other))


def stack_kernel(other_ref, down_ref, out_ref, sems):
    pieces, _, depth, units = other_ref.shape
    rest = units - depth
    pairs = [(down_ref, out_ref.at[pl.ds(0, units)])]
    for i in range(pieces):
        pairs.append(
            (other_ref.at[i, 2, :, pl.ds(0, depth)], out_ref.at[pl.ds(units, depth), pl.ds(i * depth, depth)])
        )
        for j in range(0, depth, rest):
            pairs.append(
                (
                    other_ref.at[i, 2, pl.ds(j, rest), pl.ds(depth, rest)],
                    out_ref.at[pl.ds(units + depth, rest), pl.ds(i * depth + j, rest)],
                )
            )
    copies = [pltpu.make_async_copy(a, b, sems.at[i]) for i, (a, b) in enumerate(pairs)]
    for copy in copies:
        copy.start()
    for copy in copies:
        copy.wait()


def stack(other, down):
    here = pl.BlockSpec(memory_space=pltpu.HBM)
    (pieces, _, depth, units), width = other.shape, down.shape[1]
    return pl.pallas_call(
        stack_kernel,
        in_specs=[here] * 2,
        out_specs=pl.BlockSpec(memory_space=pltpu.VMEM),
        out_shape=pltpu.VMEM((2 * units, width), jnp.bfloat16),
        scratch_shapes=[pltpu.SemaphoreType.DMA((1 + pieces * (1 + depth // (units - depth)),))],
        compiler_params=pltpu.CompilerParams(vmem_limit_bytes=VMEM_LIMIT),
        cost_estimate=pl.CostEstimate(flops=0, bytes_accessed=8 * units * width, transcendentals=0),
        name="stack",
    )(*hbm(other, down))


def expand_kernel(near_ref, near_sent_ref, far_ref, far_sent_ref, down_ref, out_ref, hidden_ref):
    units = down_ref.shape[0] // 2

    def both(mine, sent, at, size):
        at = pl.ds(at, size)
        return mine[:, at].astype(jnp.float32) + sent[:, at].astype(jnp.float32)

    total = jnp.sum(both(near_ref, near_sent_ref, 2 * units, LANES), axis=1, keepdims=True)
    scale = lax.rsqrt(total / D + EPSILON)
    kept = far_ref.shape[1] - 2 * units
    for piece, (mine, sent, at) in enumerate(((near_ref, near_sent_ref, 0), (far_ref, far_sent_ref, kept))):
        gate, up = both(mine, sent, at, units), both(mine, sent, at + units, units)
        hidden = jax.nn.silu(gate * scale) * (up * scale)
        hidden_ref[:, units * piece : units * (piece + 1)] = hidden.astype(jnp.bfloat16)
    out_ref[...] = mm(hidden_ref[...], down_ref[...]).astype(out_ref.dtype)


def expand(near, near_sent, far, far_sent, down, kind, flops):
    count, (units, width) = near.shape[0], down.shape
    vmem = pl.BlockSpec(memory_space=pltpu.VMEM)
    return pl.pallas_call(
        expand_kernel,
        in_specs=[vmem] * 5,
        out_specs=vmem,
        out_shape=jax.ShapeDtypeStruct((count, width), kind),
        scratch_shapes=[pltpu.VMEM((count, units), jnp.bfloat16)],
        compiler_params=pltpu.CompilerParams(vmem_limit_bytes=VMEM_LIMIT),
        cost_estimate=pl.CostEstimate(
            flops=flops, bytes_accessed=2 * width * units, transcendentals=count * units
        ),
        name="expand",
    )(near, near_sent, far, far_sent, pltpu.with_memory_space_constraint(down, pltpu.VMEM))


def shards(states, norm_gain, expert_ids, route_gates, w_gate, w_up, w_down):
    tokens, width = states.shape
    experts = lax.axis_size("z") // 2
    replicas = lax.axis_size("y") * lax.axis_size("core")
    capacity = tokens // 2
    rows = experts * capacity

    replica = lax.axis_index("y") * lax.axis_size("core") + lax.axis_index("core")
    near = share(replica.astype(jnp.int32)[None], replicas, w_gate[0], w_up[0], w_down[0])
    near = lax.ppermute(near, "xh", SWAP)

    flight_ids = jnp.arange(experts, dtype=jnp.int32)
    matches = expert_ids[:, :, None] == flight_ids[None, None, :]
    member = jnp.any(matches, axis=1)
    weight = jnp.sum(jnp.where(matches, route_gates[:, :, None], 0.0), axis=1)
    before = jnp.tril(jnp.ones((tokens, tokens), jnp.float32), -1)
    position = jnp.dot(before, member.astype(jnp.float32)).astype(jnp.int32)
    slots = jnp.where(member, position, capacity)
    slot_ids = jnp.arange(capacity, dtype=jnp.int32)
    placed = slots.T[:, None, :] == slot_ids[None, :, None]
    placed = placed.reshape(rows, tokens)
    packed = pack(placed.astype(jnp.bfloat16), states)
    near, _ = lax.optimization_barrier((near, packed))
    other = lax.all_gather(near, ("y", "core"), axis=0)
    exchange = functools.partial(
        lax.all_to_all, axis_name="z", split_axis=0, concat_axis=0, axis_index_groups=LINES, tiled=True
    )
    first = exchange(packed.reshape(experts, capacity, width)).reshape(rows, width)
    second = lax.ppermute(first, "z", PAIRS)

    gain = norm_gain[None, :]
    gate, up = w_gate[0], w_up[0]
    scaled1, near1, weights = project_near(first, gain, gate, up, SCALE_FLOPS)
    near_sent1 = lax.ppermute(near1, "xl", SWAP)
    near_sent1, second = lax.optimization_barrier((near_sent1, second))
    scaled2, near2 = project_again(second, gain, weights)
    far1, early, late = project_far(scaled1, scaled2, near2, other)
    early_sent = lax.ppermute(early, "xl", SWAP)
    late_sent = lax.ppermute(late, "xl", SWAP)
    other, _ = lax.optimization_barrier((other, early))
    down = stack(other, w_down[0])
    outs = [expand(early, early_sent, early, early_sent, down, jnp.bfloat16, EXPAND_FLOPS)]
    far1, _ = lax.optimization_barrier((far1, outs[0]))
    far_sent1 = lax.ppermute(far1, "xl", SWAP)
    outs.append(expand(late, late_sent, late, late_sent, down, jnp.bfloat16, EXPAND_FLOPS))
    out1 = expand(near1, near_sent1, far1, far_sent1, down, jnp.bfloat16, WAIT_FLOPS)
    back = jnp.concatenate([lax.ppermute(x, "z", PAIRS) for x in outs])
    out = (out1.astype(jnp.float32) + back.astype(jnp.float32)).astype(jnp.bfloat16)
    returned = exchange(out.reshape(experts, capacity, width)).reshape(rows, width)

    weighted = jnp.where(placed, jnp.repeat(weight.T, capacity, axis=0), 0.0)
    high = weighted.astype(jnp.bfloat16)
    low = (weighted - high.astype(jnp.float32)).astype(jnp.bfloat16)
    both = lax.dot_general(
        jnp.concatenate([high, low], axis=1),
        returned,
        (((0,), (0,)), ((), ())),
        preferred_element_type=jnp.float32,
    )
    return (both[:tokens] + both[tokens:]).astype(jnp.bfloat16)


def solution(mesh):
    dp, expert, tensor = (mesh.shape[name] for name in ("dp", "expert", "tensor"))
    fine = Mesh(
        mesh.devices.reshape(dp // 2, 2, expert // 2, 2, tensor),
        ("y", "core", "z", "xh", "xl"),
    )
    tokens, slices = ("y", "core", "z", "xh"), ("z", "xh")
    return jax.shard_map(
        shards,
        mesh=fine,
        in_specs=(
            P(tokens, "xl"),
            P("xl"),
            P(tokens, None),
            P(tokens, None),
            P(slices, "xl", None),
            P(slices, "xl", None),
            P(slices, None, "xl"),
        ),
        out_specs=P(tokens, "xl"),
        check_vma=False,
    )
```
